256 devices in a mesh: row: 16 (over x, y), col: 8 (over z), rep: 2 (over core).
Axes of the slice: x: 4, y: 4, z: 8, core: 2. Of those that a mesh axis runs over, the one named last changes fastest.
Arguments:
- amplitudes: bfloat16 [16, 2048, 2048], P('row', 'col'), may hold values from -6 to 6
- cycle_integrals: bfloat16 [4, 2048, 4, 2048], P('rep', 'col', None, 'row'), may hold values from -0.0625 to 0.0625
- ladder_integrals: bfloat16 [16, 16], replicated, may hold values from -1.5 to 1.5
- occ_energy: float32 [4], replicated, may hold values from -1.5 to -0.5
- vir_energy: float32 [2048], replicated, may hold values from 0.5 to 1.5
- occ_irrep: int32 [4], replicated, may hold values from 0 to 1
- tile_irrep: int32 [16], replicated, may hold values from 0 to 1
Outputs:
- update: float32 [4, 2048, 4, 2048], P('rep', 'col', None, 'row')
The draws below stay inside these ranges and needn't reach their ends.
All inputs are finite; a program needn't handle non-finite values.
Results may differ from the reference program's by a relative error of at most 0.0003.
Values may be sent and summed in bfloat16 or wider, within the bound.
No kernel may reach another device: no remote copies, remote signals or barrier semaphores. Data moves between devices by JAX's collectives and lax.ppermute only.
A program may use at most 64 MiB of HBM per device.

```python
import jax
import jax.numpy as jnp

NOCC = 4
NV = 2048
TILE = 128
NTILE = 16
PAIRS = 16


def touch_ends(array, own_key, least, high):
    longest = array.shape.index(max(array.shape))
    spots = []
    for shift in (0, 1):
        where = [jax.random.randint(jax.random.fold_in(own_key, axis), (), 0, length) for axis, length in enumerate(array.shape)]
        where[longest] = (where[longest] + shift) % array.shape[longest]
        spots.append(tuple(where))
    return array.at[spots[0]].set(least).at[spots[1]].set(high)


def steps_of(stream_key, dims, split, low, high):
    factor_of = 1.0
    for axis_at, parts in split:
        steps = jax.random.uniform(jax.random.fold_in(jax.random.fold_in(stream_key, 6), axis_at), (parts,), jnp.float32, low / len(split), high / len(split))
        factor_of = factor_of * jnp.repeat(jnp.exp(steps), dims[axis_at] // parts).reshape((-1,) + (1,) * (len(dims) - 1 - axis_at))
    return factor_of


def normal_values(stream_key, shape, deviation, bound, cuts=(), held_as=jnp.bfloat16):
    values = deviation * jax.random.normal(stream_key, shape, jnp.float32)
    if cuts:
        values = values * steps_of(stream_key, shape, cuts, -0.22, 0.18)
    return jnp.clip(values, -bound, bound).astype(held_as)


def setup_inputs(seed: int = 0) -> dict:
    key_list = jax.random.split(jax.random.key(seed), 8)
    return {
        "amplitudes": normal_values(key_list[0], (PAIRS, NV, NV), 1.0, 6.0, ((0, 16), (1, 8))),
        "cycle_integrals": normal_values(key_list[1], (NOCC, NV, NOCC, NV), (NOCC * NV) ** -0.5, 0.0625, ((0, 2), (1, 8), (3, 16))),
        "ladder_integrals": normal_values(key_list[2], (PAIRS, PAIRS), PAIRS ** -0.5, 1.5),
        "occ_energy": jnp.clip(jax.random.uniform(key_list[3], (NOCC,), jnp.float32, -1.5, -0.5), -1.5, -0.5),
        "vir_energy": jnp.clip(jax.random.uniform(key_list[4], (NV,), jnp.float32, 0.5, 1.5), 0.5, 1.5),
        "occ_irrep": touch_ends(jax.random.randint(key_list[5], (NOCC,), 0, 2), jax.random.fold_in(key_list[5], 1), 0, 1).astype(jnp.int32),
        "tile_irrep": touch_ends(jax.random.randint(key_list[6], (NTILE,), 0, 2), jax.random.fold_in(key_list[6], 1), 0, 1).astype(jnp.int32),
    }


def symmetry_allowed(occ_irrep, tile_irrep):
    virtual = tile_irrep[jnp.arange(NV, dtype=jnp.int32) // TILE]
    parity = occ_irrep[:, None, None, None] + occ_irrep[None, :, None, None] + virtual[None, None, :, None] + virtual[None, None, None, :]
    return parity % 2 == 0


def reference(amplitudes, cycle_integrals, ladder_integrals, occ_energy, vir_energy, occ_irrep, tile_irrep):
    allowed = symmetry_allowed(occ_irrep, tile_irrep)
    masked = jnp.where(allowed, amplitudes.reshape(NOCC, NOCC, NV, NV), jnp.zeros((), amplitudes.dtype))
    ladder = jnp.dot(ladder_integrals, masked.reshape(NOCC * NOCC, NV * NV), preferred_element_type=jnp.float32)
    ladder = ladder.reshape(NOCC, NOCC, NV, NV).transpose(0, 2, 1, 3)
    left = masked.transpose(0, 2, 1, 3).reshape(NOCC * NV, NOCC * NV)
    cycle = jnp.dot(left, cycle_integrals.reshape(NOCC * NV, NOCC * NV), preferred_element_type=jnp.float32)
    cycle = cycle.reshape(NOCC, NV, NOCC, NV)
    denom = occ_energy[:, None, None, None] - vir_energy[None, :, None, None] + occ_energy[None, None, :, None] - vir_energy[None, None, None, :]
    total = ladder + cycle
    return jnp.where(allowed.transpose(0, 2, 1, 3), total / denom, jnp.zeros((), total.dtype))
```

```python
import functools

import jax
import jax.numpy as jnp
from jax import lax
from jax.experimental import pallas as pl
from jax.experimental.pallas import tpu as pltpu
from jax.sharding import PartitionSpec as P

TILE = 128
NX, NY, NZ, NC = 4, 4, 8, 2
NOCC, NTILE = 4, 16
AXES = ("row", "col", "rep")
VMEM_LIMIT = 56 * 1024 * 1024
OCC, TILES, PX, PY, PZ, PC = 0, 4, 20, 21, 22, 23


def permutation(target):
    pairs = []
    for x in range(NX):
        for y in range(NY):
            for z in range(NZ):
                for c in range(NC):
                    tx, ty, tz, tc = target(x, y, z, c)
                    source = ((x * NY + y) * NZ + z) * NC + c
                    pairs.append((source, (((tx % NX) * NY + ty % NY) * NZ + tz % NZ) * NC + tc % NC))
    return pairs


def first_phase(v, step):
    return lax.ppermute(
        v, AXES, permutation(lambda x, y, z, c: (x, y + step, z, c) if c == 0 else (x + step, y, z, c))
    )


def second_phase(v, step):
    return lax.ppermute(
        v, AXES, permutation(lambda x, y, z, c: (x + step, y, z, c) if c == 0 else (x, y + step, z, c))
    )


def along_z(v):
    return lax.ppermute(v, AXES, permutation(lambda x, y, z, c: (x, y, z + 1 - 2 * c, c)))


def swap(v):
    return lax.ppermute(v, AXES, permutation(lambda x, y, z, c: (x, y, z, 1 - c)))


def parity(value):
    return lax.rem(value, 2)


def odd_tiles(ints):
    total = ints[TILES]
    for tile in range(1, NTILE):
        total = total + ints[TILES + tile]
    return total


def count_of(odd, which):
    return jnp.where(which == 1, odd, NTILE - odd)


def aligned(start):
    return pl.ds(pl.multiple_of(start * TILE, TILE), TILE)


OFFSETS = (0, 3, 1, 2)


def pack_kernel(cap, ints, own, ahead, behind, far, out):
    core = ints[PC]
    odd = odd_tiles(ints)
    here = jnp.where(core == 0, ints[PY], ints[PX])
    fixed = jnp.where(core == 0, ints[PX], ints[PY])
    side = ints[OCC + fixed] + ints[TILES + ints[PZ] * 2 + core]
    needs = [parity(side + ints[OCC + v]) for v in range(NOCC)]
    counts = [count_of(odd, need) for need in needs]
    for offset, buffer in zip(OFFSETS, (own, ahead, behind, far)):
        v = lax.rem(here + offset, 4)
        need = parity(side + ints[OCC + v])
        base = jnp.int32(0)
        for w in range(NOCC - 1):
            base = base + jnp.where(w < v, counts[w], 0)

        def step(tile, place, buffer=buffer, need=need):
            hit = ints[TILES + tile] == need

            @pl.when(hit)
            def _():
                out[:, aligned(place)] = buffer[:, aligned(tile)]

            return place + jnp.where(hit, 1, 0)

        lax.fori_loop(0, NTILE, step, base)


def pack(cap, ints, own, ahead, behind, far):
    vmem = pl.BlockSpec(memory_space=pltpu.VMEM)
    return pl.pallas_call(
        functools.partial(pack_kernel, cap),
        out_shape=jax.ShapeDtypeStruct((TILE, cap * TILE), jnp.bfloat16),
        in_specs=[pl.BlockSpec(memory_space=pltpu.SMEM)] + [vmem] * 4,
        out_specs=vmem,
        compiler_params=pltpu.CompilerParams(vmem_limit_bytes=VMEM_LIMIT),
        cost_estimate=pl.CostEstimate(flops=0, bytes_accessed=1 << 22, transcendentals=0),
    )(ints, own, ahead, behind, far)


def pack_cycle_kernel(cap_j, ints, w, out):
    core, z = ints[PC], ints[PZ]
    right = ints[TILES + ints[PX] * NY + ints[PY]]
    for k in range(2):
        for tile in range(2):
            need = parity(ints[OCC + core * 2 + k] + ints[TILES + z * 2 + tile] + right)
            out[k, tile, :, :] = jnp.zeros((TILE, cap_j * TILE), jnp.bfloat16)
            place = jnp.int32(0)
            for j in range(NOCC):
                hit = ints[OCC + j] == need

                @pl.when(hit)
                def _(place=place, j=j, k=k, tile=tile):
                    out[k, tile, :, aligned(place)] = w[k, j, tile * TILE : (tile + 1) * TILE, :]

                place = place + jnp.where(hit, 1, 0)


def pack_cycle(cap_j, ints, w):
    vmem = pl.BlockSpec(memory_space=pltpu.VMEM)
    return pl.pallas_call(
        functools.partial(pack_cycle_kernel, cap_j),
        out_shape=jax.ShapeDtypeStruct((2, 2, TILE, cap_j * TILE), jnp.bfloat16),
        in_specs=[pl.BlockSpec(memory_space=pltpu.SMEM), vmem],
        out_specs=vmem,
        compiler_params=pltpu.CompilerParams(vmem_limit_bytes=VMEM_LIMIT),
        cost_estimate=pl.CostEstimate(flops=0, bytes_accessed=1 << 20, transcendentals=0),
    )(ints, w)


CHUNK = 4
ROOM = 68


def products_kernel(
    cap, cap_j, ints, ladder, occ, vir,
    a0, a1, a2, a3p, a3m, w0, r1, s1, r2, s2, r3, s3, r4, s4,
    out, a_buf, w_buf, acc, tiles, a_table, w_table, kl_table, sems,
):
    core, z = ints[PC], ints[PZ]
    half = TILE // 2
    up = jnp.where(core == 0, 1, 0)
    copies = []

    def start(source, target):
        copy = pltpu.make_async_copy(source, target, sems.at[len(copies)])
        copy.start()
        copies.append(copy)

    slab = 8 * TILE
    start(a0, a_buf.at[0])
    start(a1, a_buf.at[3])
    start(a2, a_buf.at[1])
    start(w0, w_buf.at[pl.ds(0, slab), :])
    for s, (recv, swapped) in enumerate(((r1, s1), (r2, s2), (r3, s3)), 1):
        received_at = jnp.where(up == 1, 8 - s, s)
        swapped_at = jnp.where(up == 1, s, 8 - s)
        start(recv, w_buf.at[pl.ds(pl.multiple_of(received_at * slab, slab), slab), :])
        start(swapped, w_buf.at[pl.ds(pl.multiple_of(swapped_at * slab, slab), slab), :])
    start(r4, w_buf.at[pl.ds(pl.multiple_of(4 * slab + core * (slab // 2), slab // 2), slab // 2), :])
    start(s4, w_buf.at[pl.ds(pl.multiple_of(4 * slab + (1 - core) * (slab // 2), slab // 2), slab // 2), :])
    start(a3p, a_buf.at[2, pl.ds(0, half), :])
    start(a3m, a_buf.at[2, pl.ds(half, half), :])
    a_buf[4, :, 0:TILE] = jnp.zeros((TILE, TILE), jnp.bfloat16)

    odd = odd_tiles(ints)
    tile_a = ints[TILES + z * 2 + core]
    tile_b_at = ints[PX] * NY + ints[PY]
    tile_b = ints[TILES + tile_b_at]
    here = jnp.where(core == 0, ints[PX], ints[PY])
    occ_irreps = [ints[OCC + k] for k in range(NOCC)]

    lengths = []
    for g in range(2):
        place = jnp.int32(g * ROOM)
        for k in range(NOCC):
            need = parity(occ_irreps[k] + g)

            def step(tile, place, k=k, need=need):
                slot = lax.rem(lax.div(tile, 2) - z + 8, 8)
                w_table[place] = slot * 8 + k * 2 + lax.rem(tile, 2)
                return place + jnp.where(ints[TILES + tile] == need, 1, 0)

            place = lax.fori_loop(0, NTILE, step, place)
        for extra in range(CHUNK):
            w_table[place + extra] = 0
        lengths.append(place - g * ROOM)

    def entry(i, k):
        offset = jnp.int32(0)
        oi, ok = ints[OCC + i], ints[OCC + k]
        for v in range(NOCC - 1):
            with_i = count_of(odd, parity(oi + occ_irreps[v] + tile_a))
            with_k = count_of(odd, parity(ok + occ_irreps[v] + tile_a))
            offset = offset + jnp.where(core == 0, jnp.where(v < k, with_i, 0), jnp.where(v < i, with_k, 0))
        slot = lax.rem(jnp.where(core == 0, i, k) - here + 4, 4)
        return slot, offset

    for i in range(NOCC):
        place = jnp.int32(i * ROOM)
        for k in range(NOCC):
            slot, offset = entry(i, k)
            count = count_of(odd, parity(occ_irreps[i] + occ_irreps[k] + tile_a))

            def step(n, carry, place=place, first=slot * 64 + offset):
                a_table[place + n] = first + n
                return carry

            lax.fori_loop(0, count, step, 0)
            place = place + count
        for extra in range(CHUNK):
            a_table[place + extra] = 4 * 64

    rank = jnp.int32(0)
    for tile in range(NTILE - 1):
        rank = rank + jnp.where((tile < tile_b_at) & (ints[TILES + tile] == tile_b), 1, 0)

    for copy in copies:
        copy.wait()

    kl_count = jnp.int32(0)
    for k in range(NOCC):
        for l in range(NOCC):
            hit = parity(occ_irreps[k] + occ_irreps[l] + tile_a) == tile_b

            @pl.when(hit)
            def _(k=k, l=l, kl_count=kl_count):
                slot, offset = entry(k, l)
                tiles[kl_count] = a_buf[slot, :, aligned(offset + rank)].astype(jnp.float32)
                kl_table[kl_count] = k * NOCC + l

            kl_count = kl_count + jnp.where(hit, 1, 0)

    vir_b = vir[pl.ds(tile_b_at, 1), :]
    vir_a = jnp.broadcast_to(vir[pl.ds(z * 2 + core, 1), :], (TILE, TILE)).T

    for h in range(2):
        for ii in range(2):
            i = jnp.where(h == 0, core, 1 - core) * 2 + ii
            g = parity(ints[OCC + i] + tile_a)
            length = jnp.where(g == 0, lengths[0], lengths[1])

            def step(n, total, i=i, g=g):
                lefts, rights = [], []
                for part in range(CHUNK):
                    at = a_table[i * ROOM + n * CHUNK + part]
                    lefts.append(a_buf[lax.div(at, 64), :, aligned(lax.rem(at, 64))])
                    rights.append(w_buf[aligned(w_table[g * ROOM + n * CHUNK + part]), :])
                return total + jnp.dot(
                    jnp.concatenate(lefts, axis=1),
                    jnp.concatenate(rights, axis=0),
                    preferred_element_type=jnp.float32,
                )

            acc[...] = lax.fori_loop(
                0, lax.div(length + CHUNK - 1, CHUNK), step, jnp.zeros((TILE, cap_j * TILE), jnp.float32)
            )
            need = parity(g + tile_b)
            place = jnp.int32(0)
            for j in range(NOCC):
                hit = occ_irreps[j] == need

                @pl.when(hit)
                def _(i=i, j=j, h=h, ii=ii, place=place):
                    def add(n, total):
                        return total + ladder[(i * NOCC + j) * 16 + kl_table[n]] * tiles[n]

                    total = lax.fori_loop(0, kl_count, add, jnp.zeros((TILE, TILE), jnp.float32))
                    denom = ((occ[i] - vir_a) + occ[j]) - vir_b
                    out[h, ii, :, j, :] = (total + acc[:, aligned(place)]) / denom

                @pl.when(jnp.logical_not(hit))
                def _(j=j, h=h, ii=ii):
                    out[h, ii, :, j, :] = jnp.zeros((TILE, TILE), jnp.float32)

                place = place + jnp.where(hit, 1, 0)


def products(cap, cap_j, ints, ladder, occ, vir, a_blocks, w_blocks):
    vmem = pl.BlockSpec(memory_space=pltpu.VMEM)
    smem = pl.BlockSpec(memory_space=pltpu.SMEM)
    blocks = list(a_blocks) + list(w_blocks)
    return pl.pallas_call(
        functools.partial(products_kernel, cap, cap_j),
        out_shape=jax.ShapeDtypeStruct((2, 2, TILE, NOCC, TILE), jnp.float32),
        in_specs=[smem, smem, smem, vmem] + [pl.BlockSpec(memory_space=pl.ANY)] * len(blocks),
        out_specs=vmem,
        scratch_shapes=[
            pltpu.VMEM((5, TILE, cap * TILE), jnp.bfloat16),
            pltpu.VMEM((64 * TILE, cap_j * TILE), jnp.bfloat16),
            pltpu.VMEM((TILE, cap_j * TILE), jnp.float32),
            pltpu.VMEM((16, TILE, TILE), jnp.float32),
            pltpu.SMEM((NOCC * ROOM,), jnp.int32),
            pltpu.SMEM((2 * ROOM,), jnp.int32),
            pltpu.SMEM((16,), jnp.int32),
            pltpu.SemaphoreType.DMA((len(blocks),)),
        ],
        compiler_params=pltpu.CompilerParams(vmem_limit_bytes=VMEM_LIMIT),
        cost_estimate=pl.CostEstimate(flops=1 << 30, bytes_accessed=10 << 20, transcendentals=0),
    )(ints, ladder, occ, vir, *blocks)


def planned(cap, cap_j, ints, amplitudes, cycle_integrals, ladder, occ, vir):
    core = lax.axis_index("rep")
    own = lax.dynamic_slice_in_dim(amplitudes[0], core * TILE, TILE, 0)
    ahead, behind, far = first_phase(own, 1), first_phase(own, -1), first_phase(own, 2)

    mine = pack_cycle(cap_j, ints, cycle_integrals.transpose(0, 2, 1, 3))
    other = swap(mine)
    w_block = jnp.where(core == 0, jnp.concatenate([mine, other]), jnp.concatenate([other, mine]))
    w_block = w_block.reshape(8 * TILE, cap_j * TILE)
    w_blocks = [w_block]
    moving = w_block
    for _ in range(3):
        moving = along_z(moving)
        w_blocks += [moving, swap(moving)]
    last = along_z(lax.dynamic_slice_in_dim(moving, core * 4 * TILE, 4 * TILE, 0))
    w_blocks += [last, swap(last)]

    packed = pack(cap, ints, own, ahead, behind, far)
    a_ahead, a_behind = second_phase(packed, 1), second_phase(packed, -1)
    half = TILE // 2
    far_ahead, far_behind = second_phase(a_ahead[:half], 1), second_phase(a_behind[half:], -1)

    out = products(cap, cap_j, ints, ladder, occ, vir, (packed, a_ahead, a_behind, far_ahead, far_behind), w_blocks)
    kept, sent = out[0], out[1]
    came = swap(sent)
    return jnp.where(
        core == 0, jnp.concatenate([kept, came], axis=1), jnp.concatenate([came, kept], axis=1)
    )


def body(
    amplitudes, cycle_integrals, ladder_integrals, occ_energy, vir_energy, occ_irrep, tile_irrep
):
    row, z, core = (lax.axis_index(axis) for axis in AXES)
    places = jnp.stack([row // NY, row % NY, z, core]).astype(jnp.int32)
    ints = jnp.concatenate([occ_irrep, tile_irrep, places])
    ladder = ladder_integrals.astype(jnp.float32).reshape(-1)
    vir = vir_energy.reshape(NTILE, TILE)
    lean = jnp.abs(jnp.sum(occ_irrep) - 2)
    return lax.switch(
        lean,
        [functools.partial(planned, 16 * n, n) for n in (2, 3, 4)],
        ints, amplitudes, cycle_integrals, ladder, occ_energy, vir,
    )


def solution(mesh):
    in_specs = (P("row", "col", None), P("rep", "col", None, "row"), P(), P(), P(), P(), P())
    out_specs = P("rep", "col", None, "row")
    return jax.shard_map(body, mesh=mesh, in_specs=in_specs, out_specs=out_specs, check_vma=False)
```

```python
import functools

import jax
import jax.numpy as jnp
from jax import lax
from jax.experimental import pallas as pl
from jax.experimental.pallas import tpu as pltpu
from jax.sharding import PartitionSpec as P

TILE = 128
NX, NY, NZ, NC = 4, 4, 8, 2
NOCC, NTILE = 4, 16
AXES = ("row", "col", "rep")
OCC, TILES, PX, PY, PZ, PC = 0, 4, 20, 21, 22, 23
ORDER, KL_COUNT, LENGTHS, LEAN, KL, TILE_LIST = 24, 28, 29, 31, 32, 48
FAR_FIRST, FAR_START, FAR_COUNT, FAR_I = 80, 84, 86, 88
ROOM = 64
W_LISTS, A_LISTS = 128, 256
NONE = 3 * ROOM
CHUNK = 8


def permutation(target):
    pairs = []
    for x in range(NX):
        for y in range(NY):
            for z in range(NZ):
                for c in range(NC):
                    tx, ty, tz, tc = target(x, y, z, c)
                    source = ((x * NY + y) * NZ + z) * NC + c
                    pairs.append((source, (((tx % NX) * NY + ty % NY) * NZ + tz % NZ) * NC + tc % NC))
    return pairs


def first_phase(v, step):
    return lax.ppermute(
        v, AXES, permutation(lambda x, y, z, c: (x, y + step, z, c) if c == 0 else (x + step, y, z, c))
    )


def second_phase(v, step):
    return lax.ppermute(
        v, AXES, permutation(lambda x, y, z, c: (x + step, y, z, c) if c == 0 else (x, y + step, z, c))
    )


def along_z(v):
    return lax.ppermute(v, AXES, permutation(lambda x, y, z, c: (x, y, z + 1 - 2 * c, c)))


def swap(v):
    return lax.ppermute(v, AXES, permutation(lambda x, y, z, c: (x, y, z, 1 - c)))


def parity(value):
    return lax.rem(value, 2)


def odd_tiles(ints):
    total = ints[TILES]
    for tile in range(1, NTILE):
        total = total + ints[TILES + tile]
    return total


def count_of(odd, which):
    return jnp.where(which == 1, odd, NTILE - odd)


def aligned(start):
    return pl.ds(pl.multiple_of(start * TILE, TILE), TILE)


OFFSETS = (0, 3, 1, 2)


def places_kernel(occ_irrep, tile_irrep, ints):
    row, z, core = (lax.axis_index(axis) for axis in AXES)
    for at, place in ((PX, lax.div(row, NY)), (PY, lax.rem(row, NY)), (PZ, z), (PC, core)):
        ints[at] = place
    total = jnp.int32(-2)
    for k in range(NOCC):
        ints[OCC + k] = occ_irrep[k]
        total = total + occ_irrep[k]
    for tile in range(NTILE):
        ints[TILES + tile] = tile_irrep[tile]
    ints[LEAN] = jnp.abs(total)


def make_places(occ_irrep, tile_irrep):
    smem = pl.BlockSpec(memory_space=pltpu.SMEM)
    return pl.pallas_call(
        places_kernel,
        out_shape=jax.ShapeDtypeStruct((LEAN + 1,), jnp.int32),
        in_specs=[smem, smem],
        out_specs=smem,
    )(occ_irrep, tile_irrep)


def tables_kernel(places, ints):
    x, y, z, core = places[PX], places[PY], places[PZ], places[PC]
    row = x * NY + y
    for at in (PX, PY, PZ, PC, OCC, OCC + 1, OCC + 2, OCC + 3):
        ints[at] = places[at]
    occ_irreps = [places[OCC + k] for k in range(NOCC)]
    common_sum = occ_irreps[0] + occ_irreps[1] + occ_irreps[2] + occ_irreps[3]

    def list_step(tile, ends):
        even, odd = ends
        is_odd = places[TILES + tile]
        ints[TILES + tile] = is_odd
        ints[TILE_LIST + jnp.where(is_odd == 1, odd, even)] = tile
        return even + 1 - is_odd, odd + is_odd

    _, last = lax.fori_loop(0, NTILE, list_step, (jnp.int32(0), jnp.int32(NTILE)))
    odd = last - NTILE
    tile_a = places[TILES + z * 2 + core]
    tile_b = places[TILES + row]
    here = jnp.where(core == 0, x, y)
    far = lax.rem(here + 2, 4)
    ints[FAR_I] = far

    def piece_of(distance, own_half):
        below = distance > 4
        steps = jnp.where(below, 8 - distance, distance)
        received = below == (core == 0)
        part = jnp.where(received, 1 - own_half, own_half)
        ring = jnp.where(steps == 3, jnp.where(received, 10, 13), jnp.where(received, 0, 4) + steps * 2) + part
        return jnp.where(distance == 0, 1 - own_half, jnp.where(distance == 4, 15 - 3 * own_half, ring))

    for g in range(2):
        place = jnp.int32(0)
        far_start, far_count = jnp.int32(0), jnp.int32(0)
        for k in range(NOCC):
            need = parity(occ_irreps[k] + g)
            count = count_of(odd, need)
            own_half = jnp.where(core == k // 2, 1, 0)
            far_start = jnp.where(far == k, place, far_start)
            far_count = jnp.where(far == k, count, far_count)

            def step(n, carry, place=place, first=need * NTILE, own_half=own_half, k=k, g=g):
                tile = ints[TILE_LIST + first + n]
                distance = lax.rem(lax.div(tile, 2) - z + 8, 8)
                slab = piece_of(distance, own_half) * 4 + (k % 2) * 2 + lax.rem(tile, 2)
                ints[W_LISTS + g * ROOM + place + n] = slab
                return carry

            lax.fori_loop(0, count, step, 0)
            place = place + count
        ints[LENGTHS + g] = place
        ints[FAR_START + g] = jnp.where(core == 0, 0, far_start)
        ints[FAR_COUNT + g] = jnp.where(core == 0, place, far_count)

        def clear(n, carry, g=g):
            ints[W_LISTS + g * ROOM + n] = 0
            return carry

        lax.fori_loop(place, ROOM, clear, 0)

    def entry(i, k):
        offset = jnp.int32(0)
        oi, ok = ints[OCC + i], ints[OCC + k]
        for v in range(NOCC - 1):
            with_i = count_of(odd, parity(oi + occ_irreps[v] + tile_a))
            with_k = count_of(odd, parity(ok + occ_irreps[v] + tile_a))
            offset = offset + jnp.where(core == 0, jnp.where(v < k, with_i, 0), jnp.where(v < i, with_k, 0))
        distance = lax.rem(jnp.where(core == 0, i, k) - here + 4, 4)
        block = jnp.where(distance == 0, 0, jnp.where(distance == 3, 1, jnp.where(distance == 1, 2, 3)))
        return block * ROOM + offset

    rank = jnp.int32(0)
    for tile in range(NTILE - 1):
        rank = rank + jnp.where((tile < row) & (places[TILES + tile] == tile_b), 1, 0)

    def fill(i, kl_count):
        place = jnp.int32(0)
        far_first = jnp.int32(0)
        for k in range(NOCC):
            first = entry(i, k)
            need = parity(ints[OCC + i] + occ_irreps[k] + tile_a)
            count = count_of(odd, need)
            far_first = jnp.where((far == k) & (core == 1), first - NONE, far_first)

            def step(n, carry, place=place, first=first):
                ints[A_LISTS + i * ROOM + place + n] = first + n
                return carry

            lax.fori_loop(0, count, step, 0)
            place = place + count
            hit = need == tile_b

            @pl.when(hit)
            def _(first=first, k=k, kl_count=kl_count):
                ints[KL + kl_count] = (i * NOCC + k) * 256 + first + rank

            kl_count = kl_count + jnp.where(hit, 1, 0)
        ints[FAR_FIRST + i] = far_first

        def clear(n, carry):
            ints[A_LISTS + i * ROOM + n] = NONE
            return carry

        lax.fori_loop(place, ROOM, clear, 0)
        return kl_count

    ints[KL_COUNT] = lax.fori_loop(0, NOCC, fill, jnp.int32(0))
    common = jnp.where(common_sum > 2, 1, 0)
    place = jnp.int32(0)
    for irrep in (common, 1 - common):
        for i in range(NOCC):
            hit = occ_irreps[i] == irrep

            @pl.when(hit)
            def _(place=place, i=i):
                ints[ORDER + place] = i

            place = place + jnp.where(hit, 1, 0)


def make_tables(places):
    smem = pl.BlockSpec(memory_space=pltpu.SMEM)
    return pl.pallas_call(
        tables_kernel,
        out_shape=jax.ShapeDtypeStruct((A_LISTS + NOCC * ROOM,), jnp.int32),
        in_specs=[smem],
        out_specs=smem,
    )(places)


def pack_kernel(ints, own, ahead, behind, far, out):
    core = ints[PC]
    odd = odd_tiles(ints)
    here = jnp.where(core == 0, ints[PY], ints[PX])
    fixed = jnp.where(core == 0, ints[PX], ints[PY])
    side = ints[OCC + fixed] + ints[TILES + ints[PZ] * 2 + core]
    counts = [count_of(odd, parity(side + ints[OCC + v])) for v in range(NOCC)]
    for offset, buffer in zip(OFFSETS, (own, ahead, behind, far)):
        v = lax.rem(here + offset, 4)
        need = parity(side + ints[OCC + v])
        base = jnp.int32(0)
        for w in range(NOCC - 1):
            base = base + jnp.where(w < v, counts[w], 0)

        def step(n, carry, buffer=buffer, base=base, first=need * NTILE):
            out[:, aligned(base + n)] = buffer[:, aligned(ints[TILE_LIST + first + n])]
            return carry

        lax.fori_loop(0, count_of(odd, need), step, 0)


def pack(cap, ints, own, ahead, behind, far):
    vmem = pl.BlockSpec(memory_space=pltpu.VMEM)
    return pl.pallas_call(
        pack_kernel,
        out_shape=jax.ShapeDtypeStruct((TILE, cap * TILE), jnp.bfloat16),
        in_specs=[pl.BlockSpec(memory_space=pltpu.SMEM)] + [vmem] * 4,
        out_specs=vmem,
        compiler_params=pltpu.CompilerParams(vmem_limit_bytes=8 << 20),
        cost_estimate=pl.CostEstimate(flops=1 << 20, bytes_accessed=1 << 16, transcendentals=0),
    )(ints, own, ahead, behind, far)


def pack_cycle_kernel(cap_j, ints, w, out):
    core, z = ints[PC], ints[PZ]
    right = ints[TILES + ints[PX] * NY + ints[PY]]
    for k in range(2):
        for tile in range(2):
            need = parity(ints[OCC + core * 2 + k] + ints[TILES + z * 2 + tile] + right)
            rows = slice((k * 2 + tile) * TILE, (k * 2 + tile + 1) * TILE)
            if cap_j > 2:
                out[rows, :] = jnp.zeros((TILE, cap_j * TILE), jnp.bfloat16)
            place = jnp.int32(0)
            for j in range(NOCC):
                hit = ints[OCC + j] == need

                @pl.when(hit)
                def _(place=place, j=j, k=k, tile=tile, rows=rows):
                    out[rows, aligned(place)] = w[k, j, tile * TILE : (tile + 1) * TILE, :]

                place = place + jnp.where(hit, 1, 0)


def pack_cycle(cap_j, ints, w):
    vmem = pl.BlockSpec(memory_space=pltpu.VMEM)
    return pl.pallas_call(
        functools.partial(pack_cycle_kernel, cap_j),
        out_shape=jax.ShapeDtypeStruct((4 * TILE, cap_j * TILE), jnp.bfloat16),
        in_specs=[pl.BlockSpec(memory_space=pltpu.SMEM), vmem],
        out_specs=vmem,
        compiler_params=pltpu.CompilerParams(vmem_limit_bytes=4 << 20),
    )(ints, w)


def near_kernel(cap_j, ints, a_near, w_all, acc):
    def product(rows):
        g = parity(ints[OCC + rows[0]] + ints[TILES + ints[PZ] * 2 + ints[PC]])

        def a_tile(i, n):
            at = ints[A_LISTS + i * ROOM + n]
            block = lax.div(at, ROOM)
            tile = a_near[aligned(jnp.minimum(block, 2)), aligned(jnp.where(block == 3, 0, lax.rem(at, ROOM)))]
            return jnp.where(block == 3, jnp.zeros_like(tile), tile)

        def step(n, total):
            lefts, rights = [], []
            for part in range(CHUNK):
                at = n * CHUNK + part
                lefts.append(jnp.concatenate([a_tile(i, at) for i in rows], axis=0))
                rights.append(w_all[aligned(ints[W_LISTS + g * ROOM + at]), :])
            return total + jnp.dot(
                jnp.concatenate(lefts, axis=1),
                jnp.concatenate(rights, axis=0),
                preferred_element_type=jnp.float32,
            )

        total = lax.fori_loop(
            0,
            lax.div(ints[LENGTHS + g] + CHUNK - 1, CHUNK),
            step,
            jnp.zeros((len(rows) * TILE, cap_j * TILE), jnp.float32),
        )
        for at, i in enumerate(rows):
            acc[i] = total[at * TILE : (at + 1) * TILE]

    for_groups(cap_j, ints, product)


def for_groups(cap_j, ints, product):
    def single(n, carry):
        product([ints[ORDER + n]])
        return carry

    def pair(n, carry):
        product([ints[ORDER + 2 * n], ints[ORDER + 2 * n + 1]])
        return carry

    if cap_j == 2:
        lax.fori_loop(0, 2, pair, 0)
    else:
        product([ints[ORDER], ints[ORDER + 1]])
        lax.fori_loop(2, NOCC, single, 0)


def far_kernel(cap_j, ints, ladder, occ, vir, a_near, a_far, w_all, acc_in, kept, sent, acc, tiles):
    core, z = ints[PC], ints[PZ]
    tile_a_at, tile_b_at = z * 2 + core, ints[PX] * NY + ints[PY]
    tile_a, tile_b = ints[TILES + tile_a_at], ints[TILES + tile_b_at]
    occ_irreps = [ints[OCC + k] for k in range(NOCC)]
    acc[...] = acc_in[...]

    def product(rows):
        g = parity(ints[OCC + rows[0]] + tile_a)
        first, count = ints[FAR_START + g], ints[FAR_COUNT + g]

        def add(begin, size):
            lefts, rights = [], []
            for part in range(size):
                lefts.append(
                    jnp.concatenate([a_far[:, aligned(ints[FAR_FIRST + i] + begin + part)] for i in rows], axis=0)
                )
                rights.append(w_all[aligned(ints[W_LISTS + g * ROOM + first + begin + part]), :])
            total = jnp.dot(
                jnp.concatenate(lefts, axis=1),
                jnp.concatenate(rights, axis=0),
                preferred_element_type=jnp.float32,
            )
            for at, i in enumerate(rows):
                acc[i] += total[at * TILE : (at + 1) * TILE]

        whole = lax.div(count, 4)

        def by_four(n, carry):
            add(n * 4, 4)
            return carry

        def by_one(n, carry):
            add(n, 1)
            return carry

        lax.fori_loop(0, whole, by_four, 0)
        lax.fori_loop(whole * 4, count, by_one, 0)

    @pl.when(core == 0)
    def _():
        product([ints[FAR_I]])

    @pl.when(core == 1)
    def _():
        for_groups(cap_j, ints, product)

    kl_count = ints[KL_COUNT]

    def keep_tile(n, carry):
        at = lax.rem(ints[KL + n], 256)
        block, columns = lax.div(at, ROOM), aligned(lax.rem(at, ROOM))
        near = a_near[aligned(jnp.minimum(block, 2)), columns]
        tiles[n] = jnp.where(block == 3, a_far[:, columns], near).astype(jnp.float32)
        return carry

    lax.fori_loop(0, kl_count, keep_tile, 0)
    vir_b = vir[pl.ds(tile_b_at, 1), :]
    vir_a = jnp.broadcast_to(vir[pl.ds(tile_a_at, 1), :], (TILE, TILE)).T

    for out, begin, at in ((kept, core * 2, core * TILE), (sent, 2 - core * 2, 0)):
        rows = pl.ds(pl.multiple_of(at, TILE), TILE)

        def finish(ii, carry, out=out, begin=begin, rows=rows):
            i = begin + ii
            need = parity(ints[OCC + i] + tile_a + tile_b)
            place = jnp.int32(0)
            for j in range(NOCC):
                hit = occ_irreps[j] == need

                @pl.when(hit)
                def _(j=j, place=place):
                    def add(n, total):
                        return total + ladder[(i * NOCC + j) * 16 + lax.div(ints[KL + n], 256)] * tiles[n]

                    total = lax.fori_loop(0, kl_count, add, acc[i, :, aligned(place)])
                    out[ii, rows, j, :] = total / (((occ[i] - vir_a) + occ[j]) - vir_b)

                @pl.when(jnp.logical_not(hit))
                def _(j=j):
                    out[ii, rows, j, :] = jnp.zeros((TILE, TILE), jnp.float32)

                place = place + jnp.where(hit, 1, 0)
            return carry

        lax.fori_loop(0, 2, finish, 0)


def products(cap, cap_j, ints, ladder, occ, vir, a_near, a_far, w_all):
    vmem = pl.BlockSpec(memory_space=pltpu.VMEM)
    smem = pl.BlockSpec(memory_space=pltpu.SMEM)
    sums = (NOCC, TILE, cap_j * TILE)
    whole = jax.ShapeDtypeStruct((2, 2 * TILE, NOCC, TILE), jnp.float32)
    half = jax.ShapeDtypeStruct((2, TILE, NOCC, TILE), jnp.float32)
    limit = (14 << 20) * cap // 32
    acc = pl.pallas_call(
        functools.partial(near_kernel, cap_j),
        out_shape=jax.ShapeDtypeStruct(sums, jnp.float32),
        in_specs=[smem, vmem, vmem],
        out_specs=vmem,
        compiler_params=pltpu.CompilerParams(vmem_limit_bytes=limit),
        cost_estimate=pl.CostEstimate(flops=1 << 20, bytes_accessed=1 << 16, transcendentals=0),
    )(ints, a_near, w_all)
    return pl.pallas_call(
        functools.partial(far_kernel, cap_j),
        out_shape=(whole, half),
        in_specs=[smem, smem, smem, vmem, vmem, vmem, vmem, vmem],
        out_specs=(vmem, vmem),
        scratch_shapes=[pltpu.VMEM(sums, jnp.float32), pltpu.VMEM((16, TILE, TILE), jnp.float32)],
        compiler_params=pltpu.CompilerParams(vmem_limit_bytes=limit + (2 << 20)),
        cost_estimate=pl.CostEstimate(flops=1 << 20, bytes_accessed=1 << 16, transcendentals=0),
    )(ints, ladder, occ, vir, a_near, a_far, w_all, acc)


def own_rows(amplitudes):
    return lax.dynamic_slice_in_dim(amplitudes[0], lax.axis_index("rep") * TILE, TILE, 0)


def planned(cap, cap_j, places, amplitudes, w, ladder, occ, vir):
    own = own_rows(amplitudes)
    ahead, behind, far = first_phase(own, 1), first_phase(own, -1), first_phase(own, 2)

    mine = pack_cycle(cap_j, places, w)
    other = swap(mine)
    ring = []
    first, second = mine, other
    ints = make_tables(places)
    for step in range(3):
        if step == 1:
            first, second, ints = lax.optimization_barrier((first, second, ints))
        first, second = along_z(first), along_z(second)
        ring += [first, second]
    ring.append(along_z(first))

    packed = pack(cap, ints, own, ahead, behind, far)
    a_near = jnp.concatenate([packed, second_phase(packed, 1), second_phase(packed, -1)])
    a_far = second_phase(packed, 2)

    near, further = jnp.concatenate(ring[:4]), jnp.concatenate(ring[4:])
    further, a_far = lax.optimization_barrier((further, a_far))
    w_all = jnp.concatenate([mine, other, near, swap(near), further, swap(further)])
    ladder = lax.optimization_barrier((ladder, packed))[0].astype(jnp.float32)
    return products(cap, cap_j, ints, ladder, occ, vir, a_near, a_far, w_all)


def general(ints, amplitudes, w, ladder, occ, vir):
    row, z, core = (lax.axis_index(axis) for axis in AXES)

    def ring(v, axis, here):
        size = lax.axis_size(axis)
        turn = [(n, (n + 1) % size) for n in range(size)]

        def step(n, carry):
            moving, held = carry
            moving = lax.ppermute(moving, axis, turn)
            return moving, lax.dynamic_update_index_in_dim(held, moving, (here - n + size) % size, 0)

        held = jnp.zeros((size,) + v.shape, v.dtype)
        held = lax.dynamic_update_index_in_dim(held, v, here, 0)
        return lax.fori_loop(1, size, step, (v, held))[1]

    tile_a, tile_b = z * 2 + core, row
    amp = ring(own_rows(amplitudes), "row", row).reshape(NOCC, NOCC, TILE, NTILE * TILE)
    other = swap(w)
    w = jnp.where(core == 0, jnp.concatenate([w, other]), jnp.concatenate([other, w]))
    w = ring(w, "col", z)
    occ_irrep, tile_irrep = ints[OCC:TILES], ints[TILES:PX]
    pairs = occ_irrep[:, None] + occ_irrep[None, :]

    def left(k, tile):
        block = lax.dynamic_slice(amp, (0, k, 0, tile * TILE), (NOCC, 1, TILE, TILE))[:, 0]
        allowed = (pairs[:, k] + tile_irrep[tile_a] + tile_irrep[tile]) % 2 == 0
        return jnp.where(allowed[:, None, None], block, jnp.zeros((), block.dtype))

    def cycle_step(n, total):
        k, tile = n // NTILE, n % NTILE
        right = lax.dynamic_slice(w, (tile // 2, k, 0, tile % 2 * TILE, 0), (1, 1, NOCC, TILE, TILE))
        return total + jnp.einsum("iac,jcb->iajb", left(k, tile), right[0, 0], preferred_element_type=jnp.float32)

    total = lax.fori_loop(0, NOCC * NTILE, cycle_step, jnp.zeros((NOCC, TILE, NOCC, TILE), jnp.float32))
    coefficients = ladder.astype(jnp.float32).reshape(NOCC, NOCC, NOCC, NOCC)

    def ladder_step(l, total):
        column = left(l, tile_b).astype(jnp.float32)
        for k in range(NOCC):
            total = total + coefficients[:, None, :, k, l, None] * column[k][None, :, None, :]
        return total

    total = lax.fori_loop(0, NOCC, ladder_step, total)
    denom = (
        occ[:, None, None, None] - vir[tile_a][:, None, None] + occ[:, None] - vir[tile_b]
    )
    kept_pairs = ((pairs + tile_irrep[tile_a] + tile_irrep[tile_b]) % 2 == 0)[:, None, :, None]
    out = jnp.where(kept_pairs, total / denom, jnp.zeros((), jnp.float32))
    kept = jnp.tile(lax.dynamic_slice_in_dim(out, core * 2, 2, 0), (1, 2, 1, 1))
    return kept, lax.dynamic_slice_in_dim(out, 2 - core * 2, 2, 0)


def body(
    amplitudes, cycle_integrals, ladder_integrals, occ_energy, vir_energy, occ_irrep, tile_irrep
):
    w = cycle_integrals.transpose(0, 2, 1, 3)
    ladder = ladder_integrals.reshape(-1)
    vir = vir_energy.reshape(NTILE, TILE)
    places = make_places(occ_irrep, tile_irrep)
    kept, sent = lax.switch(
        places[LEAN],
        [functools.partial(planned, 32, 2), functools.partial(planned, 48, 3), general],
        places, amplitudes, w, ladder, occ_energy, vir,
    )
    return lax.dynamic_update_slice_in_dim(kept, swap(sent), (1 - lax.axis_index("rep")) * TILE, 1)


def solution(mesh):
    in_specs = (P("row", "col", None), P("rep", "col", None, "row"), P(), P(), P(), P(), P())
    out_specs = P("rep", "col", None, "row")
    return jax.shard_map(body, mesh=mesh, in_specs=in_specs, out_specs=out_specs, check_vma=False)
```

```python
import functools

import jax
import jax.numpy as jnp
from jax import lax
from jax.experimental import pallas as pl
from jax.experimental.pallas import tpu as pltpu
from jax.sharding import PartitionSpec as P

TILE = 128
NX, NY, NZ, NC = 4, 4, 8, 2
NOCC, NTILE = 4, 16
AXES = ("row", "col", "rep")
OCC, TILES, PX, PY, PZ, PC = 0, 4, 20, 21, 22, 23
ORDER, KL_COUNT, LENGTHS, LEAN, KL, TILE_LIST = 24, 28, 29, 31, 32, 48
FAR_FIRST, FAR_START, FAR_COUNT, FAR_I = 80, 84, 86, 88
WINDOW = 92
ROOM = 64
W_LISTS, A_LISTS = 128, 256
NONE = 3 * ROOM
CHUNK = 8


def permutation(target):
    pairs = []
    for x in range(NX):
        for y in range(NY):
            for z in range(NZ):
                for c in range(NC):
                    tx, ty, tz, tc = target(x, y, z, c)
                    source = ((x * NY + y) * NZ + z) * NC + c
                    pairs.append((source, (((tx % NX) * NY + ty % NY) * NZ + tz % NZ) * NC + tc % NC))
    return pairs


def first_phase(v, step):
    return lax.ppermute(
        v, AXES, permutation(lambda x, y, z, c: (x, y + step, z, c) if c == 0 else (x + step, y, z, c))
    )


def second_phase(v, step):
    return lax.ppermute(
        v, AXES, permutation(lambda x, y, z, c: (x + step, y, z, c) if c == 0 else (x, y + step, z, c))
    )


def along_z(v):
    return lax.ppermute(v, AXES, permutation(lambda x, y, z, c: (x, y, z + 1 - 2 * c, c)))


def swap(v):
    return lax.ppermute(v, AXES, permutation(lambda x, y, z, c: (x, y, z, 1 - c)))


def parity(value):
    return lax.rem(value, 2)


def tiles_by_irrep(ints):
    first, end = ints[WINDOW], ints[WINDOW + 1]
    odd = jnp.int32(0)
    for tile in range(NTILE):
        odd = odd + jnp.where((tile >= first) & (tile < end), ints[TILES + tile], 0)
    return end - first - odd, odd


def count_of(counts, which):
    return jnp.where(which == 1, counts[1], counts[0])


def aligned(start):
    return pl.ds(pl.multiple_of(start * TILE, TILE), TILE)


OFFSETS = (0, 3, 1, 2)


def places_kernel(occ_irrep, tile_irrep, ints):
    row, z, core = (lax.axis_index(axis) for axis in AXES)
    for at, place in ((PX, lax.div(row, NY)), (PY, lax.rem(row, NY)), (PZ, z), (PC, core)):
        ints[at] = place
    total = jnp.int32(-2)
    for k in range(NOCC):
        ints[OCC + k] = occ_irrep[k]
        total = total + occ_irrep[k]
    for tile in range(NTILE):
        ints[TILES + tile] = tile_irrep[tile]
    ints[LEAN] = jnp.abs(total)


def make_places(occ_irrep, tile_irrep):
    smem = pl.BlockSpec(memory_space=pltpu.SMEM)
    return pl.pallas_call(
        places_kernel,
        out_shape=jax.ShapeDtypeStruct((LEAN + 1,), jnp.int32),
        in_specs=[smem, smem],
        out_specs=smem,
    )(occ_irrep, tile_irrep)


def tables_kernel(places, window, ints):
    x, y, z, core = places[PX], places[PY], places[PZ], places[PC]
    row = x * NY + y
    for at in (PX, PY, PZ, PC, OCC, OCC + 1, OCC + 2, OCC + 3):
        ints[at] = places[at]
    occ_irreps = [places[OCC + k] for k in range(NOCC)]
    common_sum = occ_irreps[0] + occ_irreps[1] + occ_irreps[2] + occ_irreps[3]

    for n in range(4):
        ints[WINDOW + n] = window[n]
    for tile in range(NTILE):
        ints[TILES + tile] = places[TILES + tile]

    def list_step(tile, ends):
        even, odd = ends
        is_odd = places[TILES + tile]
        ints[TILE_LIST + jnp.where(is_odd == 1, odd, even)] = tile
        return even + 1 - is_odd, odd + is_odd

    evens, odds = lax.fori_loop(window[0], window[1], list_step, (jnp.int32(0), jnp.int32(NTILE)))
    counts = (evens, odds - NTILE)
    tile_a = places[TILES + z * 2 + core]
    tile_b = places[TILES + row]
    here = jnp.where(core == 0, x, y)
    far = lax.rem(here + 2, 4)
    ints[FAR_I] = far

    def piece_of(distance, own_half):
        below = distance > 4
        steps = jnp.where(below, 8 - distance, distance)
        received = below == (core == 0)
        part = jnp.where(received, 1 - own_half, own_half)
        ring = jnp.where(steps == 3, jnp.where(received, 10, 13), jnp.where(received, 0, 4) + steps * 2) + part
        return jnp.where(distance == 0, 1 - own_half, jnp.where(distance == 4, 15 - 3 * own_half, ring))

    for g in range(2):
        place = jnp.int32(0)
        far_start, far_count = jnp.int32(0), jnp.int32(0)
        for k in range(NOCC):
            need = parity(occ_irreps[k] + g)
            count = count_of(counts, need)
            own_half = jnp.where(core == k // 2, 1, 0)
            far_start = jnp.where(far == k, place, far_start)
            far_count = jnp.where(far == k, count, far_count)

            def step(n, carry, place=place, first=need * NTILE, own_half=own_half, k=k, g=g):
                tile = ints[TILE_LIST + first + n]
                distance = lax.rem(lax.div(tile, 2) - z + 8, 8)
                slab = piece_of(distance, own_half) * 4 + (k % 2) * 2 + lax.rem(tile, 2)
                ints[W_LISTS + g * ROOM + place + n] = slab
                return carry

            lax.fori_loop(0, count, step, 0)
            place = place + count
        ints[LENGTHS + g] = place
        ints[FAR_START + g] = jnp.where(core == 0, 0, far_start)
        ints[FAR_COUNT + g] = jnp.where(core == 0, place, far_count)

        def clear(n, carry, g=g):
            ints[W_LISTS + g * ROOM + n] = 0
            return carry

        lax.fori_loop(place, ROOM, clear, 0)

    def entry(i, k):
        offset = jnp.int32(0)
        oi, ok = ints[OCC + i], ints[OCC + k]
        for v in range(NOCC - 1):
            with_i = count_of(counts, parity(oi + occ_irreps[v] + tile_a))
            with_k = count_of(counts, parity(ok + occ_irreps[v] + tile_a))
            offset = offset + jnp.where(core == 0, jnp.where(v < k, with_i, 0), jnp.where(v < i, with_k, 0))
        distance = lax.rem(jnp.where(core == 0, i, k) - here + 4, 4)
        block = jnp.where(distance == 0, 0, jnp.where(distance == 3, 1, jnp.where(distance == 1, 2, 3)))
        return block * ROOM + offset

    rank = jnp.int32(0)
    for tile in range(NTILE - 1):
        rank = rank + jnp.where((tile >= window[0]) & (tile < row) & (places[TILES + tile] == tile_b), 1, 0)

    def fill(i, kl_count):
        place = jnp.int32(0)
        far_first = jnp.int32(0)
        for k in range(NOCC):
            first = entry(i, k)
            need = parity(ints[OCC + i] + occ_irreps[k] + tile_a)
            count = count_of(counts, need)
            far_first = jnp.where((far == k) & (core == 1), first - NONE, far_first)

            def step(n, carry, place=place, first=first):
                ints[A_LISTS + i * ROOM + place + n] = first + n
                return carry

            lax.fori_loop(0, count, step, 0)
            place = place + count
            hit = (need == tile_b) & (row >= window[0]) & (row < window[1])

            @pl.when(hit)
            def _(first=first, k=k, kl_count=kl_count):
                ints[KL + kl_count] = (i * NOCC + k) * 256 + first + rank

            kl_count = kl_count + jnp.where(hit, 1, 0)
        ints[FAR_FIRST + i] = far_first

        def clear(n, carry):
            ints[A_LISTS + i * ROOM + n] = NONE
            return carry

        lax.fori_loop(place, ROOM, clear, 0)
        return kl_count

    ints[KL_COUNT] = lax.fori_loop(0, NOCC, fill, jnp.int32(0))
    common = jnp.where(common_sum > 2, 1, 0)
    place = jnp.int32(0)
    for irrep in (common, 1 - common):
        for i in range(NOCC):
            hit = occ_irreps[i] == irrep

            @pl.when(hit)
            def _(place=place, i=i):
                ints[ORDER + place] = i

            place = place + jnp.where(hit, 1, 0)


def make_tables(places, window):
    smem = pl.BlockSpec(memory_space=pltpu.SMEM)
    return pl.pallas_call(
        tables_kernel,
        out_shape=jax.ShapeDtypeStruct((A_LISTS + NOCC * ROOM,), jnp.int32),
        in_specs=[smem, smem],
        out_specs=smem,
    )(places, window)


def pack_kernel(ints, own, ahead, behind, far, out):
    core = ints[PC]
    tile_counts = tiles_by_irrep(ints)
    here = jnp.where(core == 0, ints[PY], ints[PX])
    fixed = jnp.where(core == 0, ints[PX], ints[PY])
    side = ints[OCC + fixed] + ints[TILES + ints[PZ] * 2 + core]
    counts = [count_of(tile_counts, parity(side + ints[OCC + v])) for v in range(NOCC)]
    for offset, buffer in zip(OFFSETS, (own, ahead, behind, far)):
        v = lax.rem(here + offset, 4)
        need = parity(side + ints[OCC + v])
        base = jnp.int32(0)
        for w in range(NOCC - 1):
            base = base + jnp.where(w < v, counts[w], 0)

        def step(n, carry, buffer=buffer, base=base, first=need * NTILE):
            out[:, aligned(base + n)] = buffer[:, aligned(ints[TILE_LIST + first + n])]
            return carry

        lax.fori_loop(0, count_of(tile_counts, need), step, 0)


def pack(cap, ints, own, ahead, behind, far):
    vmem = pl.BlockSpec(memory_space=pltpu.VMEM)
    return pl.pallas_call(
        pack_kernel,
        out_shape=jax.ShapeDtypeStruct((TILE, cap * TILE), jnp.bfloat16),
        in_specs=[pl.BlockSpec(memory_space=pltpu.SMEM)] + [vmem] * 4,
        out_specs=vmem,
        compiler_params=pltpu.CompilerParams(vmem_limit_bytes=8 << 20),
        cost_estimate=pl.CostEstimate(flops=1 << 20, bytes_accessed=1 << 16, transcendentals=0),
    )(ints, own, ahead, behind, far)


def pack_cycle_kernel(cap_j, ints, window, w, out):
    core, z = ints[PC], ints[PZ]
    right = ints[TILES + ints[PX] * NY + ints[PY]]
    for k in range(2):
        for tile in range(2):
            need = parity(ints[OCC + core * 2 + k] + ints[TILES + z * 2 + tile] + right)
            rows = slice((k * 2 + tile) * TILE, (k * 2 + tile + 1) * TILE)
            if cap_j > 2:
                out[rows, :] = jnp.zeros((TILE, cap_j * TILE), jnp.bfloat16)
            place = jnp.int32(0)
            for j in range(NOCC):
                hit = (ints[OCC + j] == need) & (j >= window[2]) & (j < window[3])

                @pl.when(hit)
                def _(place=place, j=j, k=k, tile=tile, rows=rows):
                    out[rows, aligned(place)] = w[k, j, tile * TILE : (tile + 1) * TILE, :]

                place = place + jnp.where(hit, 1, 0)


def pack_cycle(cap_j, ints, window, w):
    vmem = pl.BlockSpec(memory_space=pltpu.VMEM)
    smem = pl.BlockSpec(memory_space=pltpu.SMEM)
    return pl.pallas_call(
        functools.partial(pack_cycle_kernel, cap_j),
        out_shape=jax.ShapeDtypeStruct((4 * TILE, cap_j * TILE), jnp.bfloat16),
        in_specs=[smem, smem, vmem],
        out_specs=vmem,
        compiler_params=pltpu.CompilerParams(vmem_limit_bytes=4 << 20),
    )(ints, window, w)


def near_kernel(cap_j, ints, a_near, w_all, acc):
    def product(rows):
        g = parity(ints[OCC + rows[0]] + ints[TILES + ints[PZ] * 2 + ints[PC]])

        def a_tile(i, n):
            at = ints[A_LISTS + i * ROOM + n]
            block = lax.div(at, ROOM)
            tile = a_near[aligned(jnp.minimum(block, 2)), aligned(jnp.where(block == 3, 0, lax.rem(at, ROOM)))]
            return jnp.where(block == 3, jnp.zeros_like(tile), tile)

        def step(n, total):
            lefts, rights = [], []
            for part in range(CHUNK):
                at = n * CHUNK + part
                lefts.append(jnp.concatenate([a_tile(i, at) for i in rows], axis=0))
                rights.append(w_all[aligned(ints[W_LISTS + g * ROOM + at]), :])
            return total + jnp.dot(
                jnp.concatenate(lefts, axis=1),
                jnp.concatenate(rights, axis=0),
                preferred_element_type=jnp.float32,
            )

        total = lax.fori_loop(
            0,
            lax.div(ints[LENGTHS + g] + CHUNK - 1, CHUNK),
            step,
            jnp.zeros((len(rows) * TILE, cap_j * TILE), jnp.float32),
        )
        for at, i in enumerate(rows):
            acc[i] = total[at * TILE : (at + 1) * TILE]

    for_groups(cap_j, ints, product)


def for_groups(cap_j, ints, product):
    def single(n, carry):
        product([ints[ORDER + n]])
        return carry

    def pair(n, carry):
        product([ints[ORDER + 2 * n], ints[ORDER + 2 * n + 1]])
        return carry

    if cap_j == 2:
        lax.fori_loop(0, 2, pair, 0)
    else:
        product([ints[ORDER], ints[ORDER + 1]])
        lax.fori_loop(2, NOCC, single, 0)


def far_kernel(cap_j, ints, ladder, occ, vir, a_near, a_far, w_all, acc_in, *refs):
    earlier, (kept, sent, acc, tiles) = refs[:-4], refs[-4:]
    core, z = ints[PC], ints[PZ]
    tile_a_at, tile_b_at = z * 2 + core, ints[PX] * NY + ints[PY]
    tile_a, tile_b = ints[TILES + tile_a_at], ints[TILES + tile_b_at]
    occ_irreps = [ints[OCC + k] for k in range(NOCC)]
    acc[...] = acc_in[...]

    def product(rows):
        g = parity(ints[OCC + rows[0]] + tile_a)
        first, count = ints[FAR_START + g], ints[FAR_COUNT + g]

        def add(begin, size):
            lefts, rights = [], []
            for part in range(size):
                lefts.append(
                    jnp.concatenate([a_far[:, aligned(ints[FAR_FIRST + i] + begin + part)] for i in rows], axis=0)
                )
                rights.append(w_all[aligned(ints[W_LISTS + g * ROOM + first + begin + part]), :])
            total = jnp.dot(
                jnp.concatenate(lefts, axis=1),
                jnp.concatenate(rights, axis=0),
                preferred_element_type=jnp.float32,
            )
            for at, i in enumerate(rows):
                acc[i] += total[at * TILE : (at + 1) * TILE]

        whole = lax.div(count, 4)

        def by_four(n, carry):
            add(n * 4, 4)
            return carry

        def by_one(n, carry):
            add(n, 1)
            return carry

        lax.fori_loop(0, whole, by_four, 0)
        lax.fori_loop(whole * 4, count, by_one, 0)

    @pl.when(core == 0)
    def _():
        product([ints[FAR_I]])

    @pl.when(core == 1)
    def _():
        for_groups(cap_j, ints, product)

    kl_count = ints[KL_COUNT]

    def keep_tile(n, carry):
        at = lax.rem(ints[KL + n], 256)
        block, columns = lax.div(at, ROOM), aligned(lax.rem(at, ROOM))
        near = a_near[aligned(jnp.minimum(block, 2)), columns]
        tiles[n] = jnp.where(block == 3, a_far[:, columns], near).astype(jnp.float32)
        return carry

    lax.fori_loop(0, kl_count, keep_tile, 0)
    vir_b = vir[pl.ds(tile_b_at, 1), :]
    vir_a = jnp.broadcast_to(vir[pl.ds(tile_a_at, 1), :], (TILE, TILE)).T

    is_first = (ints[WINDOW] == 0) & (ints[WINDOW + 2] == 0)
    for side, (out, begin, at) in enumerate(((kept, core * 2, core * TILE), (sent, 2 - core * 2, 0))):
        rows = pl.ds(pl.multiple_of(at, TILE), TILE)

        def finish(ii, carry, side=side, out=out, begin=begin, rows=rows):
            i = begin + ii
            need = parity(ints[OCC + i] + tile_a + tile_b)
            place = jnp.int32(0)
            for j in range(NOCC):
                hit = (occ_irreps[j] == need) & (j >= ints[WINDOW + 2]) & (j < ints[WINDOW + 3])

                @pl.when(hit)
                def _(j=j, place=place):
                    def add(n, total):
                        return total + ladder[(i * NOCC + j) * 16 + lax.div(ints[KL + n], 256)] * tiles[n]

                    total = lax.fori_loop(0, kl_count, add, acc[i, :, aligned(place)])
                    out[ii, rows, j, :] = total / (((occ[i] - vir_a) + occ[j]) - vir_b)

                @pl.when(jnp.logical_not(hit))
                def _(j=j):
                    out[ii, rows, j, :] = jnp.zeros((TILE, TILE), jnp.float32)

                if earlier:

                    @pl.when(jnp.logical_not(is_first))
                    def _(j=j):
                        out[ii, rows, j, :] += earlier[side][ii, rows, j, :]

                place = place + jnp.where(hit, 1, 0)
            return carry

        lax.fori_loop(0, 2, finish, 0)


OUT_SHAPES = tuple(jax.ShapeDtypeStruct((2, rows, NOCC, TILE), jnp.float32) for rows in (2 * TILE, TILE))


def products(cap, cap_j, ints, ladder, occ, vir, a_near, a_far, w_all, earlier):
    vmem = pl.BlockSpec(memory_space=pltpu.VMEM)
    smem = pl.BlockSpec(memory_space=pltpu.SMEM)
    sums = (NOCC, TILE, cap_j * TILE)
    limit = (14 << 20) * cap // 32
    acc = pl.pallas_call(
        functools.partial(near_kernel, cap_j),
        out_shape=jax.ShapeDtypeStruct(sums, jnp.float32),
        in_specs=[smem, vmem, vmem],
        out_specs=vmem,
        compiler_params=pltpu.CompilerParams(vmem_limit_bytes=limit),
        cost_estimate=pl.CostEstimate(flops=1 << 20, bytes_accessed=1 << 16, transcendentals=0),
    )(ints, a_near, w_all)
    return pl.pallas_call(
        functools.partial(far_kernel, cap_j),
        out_shape=OUT_SHAPES,
        in_specs=[smem, smem, smem] + [vmem] * (5 + len(earlier)),
        out_specs=(vmem, vmem),
        scratch_shapes=[pltpu.VMEM(sums, jnp.float32), pltpu.VMEM((16, TILE, TILE), jnp.float32)],
        compiler_params=pltpu.CompilerParams(vmem_limit_bytes=limit + (4 << 20)),
        cost_estimate=pl.CostEstimate(flops=1 << 20, bytes_accessed=1 << 16, transcendentals=0),
    )(ints, ladder, occ, vir, a_near, a_far, w_all, acc, *earlier)


def own_rows(amplitudes):
    return lax.dynamic_slice_in_dim(amplitudes[0], lax.axis_index("rep") * TILE, TILE, 0)


def planned(cap, cap_j, earlier, window, places, amplitudes, w, ladder, occ, vir):
    own = own_rows(amplitudes)
    ahead, behind, far = first_phase(own, 1), first_phase(own, -1), first_phase(own, 2)

    mine = pack_cycle(cap_j, places, window, w)
    other = swap(mine)
    ring = []
    first, second = mine, other
    ints = make_tables(places, window)
    for step in range(3):
        if step == 1:
            first, second, ints = lax.optimization_barrier((first, second, ints))
        first, second = along_z(first), along_z(second)
        ring += [first, second]
    ring.append(along_z(first))

    packed = pack(cap, ints, own, ahead, behind, far)
    a_near = jnp.concatenate([packed, second_phase(packed, 1), second_phase(packed, -1)])
    a_far = second_phase(packed, 2)

    near, further = jnp.concatenate(ring[:4]), jnp.concatenate(ring[4:])
    further, a_far = lax.optimization_barrier((further, a_far))
    w_all = jnp.concatenate([mine, other, near, swap(near), further, swap(further)])
    ladder = lax.optimization_barrier((ladder, packed))[0].astype(jnp.float32)
    return products(cap, cap_j, ints, ladder, occ, vir, a_near, a_far, w_all, earlier)


def balanced(*operands):
    return planned(32, 2, (), jnp.array([0, NTILE, 0, NOCC], jnp.int32), *operands)


def unbalanced(places, *operands):
    even_split = places[LEAN] == 2

    def one_pass(n, earlier):
        c, j = n % 2 * (NTILE // 2), n // 2 * 2
        window = jnp.where(
            even_split, jnp.stack([c, c + NTILE // 2, j, j + 2]), jnp.array([0, NTILE, 0, NOCC], jnp.int32)
        )
        return planned(48, 3, earlier, window.astype(jnp.int32), places, *operands)

    space = pl.BlockSpec(memory_space=pl.ANY)
    unset = pl.pallas_call(lambda kept, sent: None, out_shape=OUT_SHAPES, out_specs=(space, space))()
    return lax.fori_loop(0, jnp.where(even_split, 4, 1), one_pass, tuple(unset))


def body(
    amplitudes, cycle_integrals, ladder_integrals, occ_energy, vir_energy, occ_irrep, tile_irrep
):
    w = cycle_integrals.transpose(0, 2, 1, 3)
    ladder = ladder_integrals.reshape(-1)
    vir = vir_energy.reshape(NTILE, TILE)
    places = make_places(occ_irrep, tile_irrep)
    kept, sent = lax.switch(
        jnp.minimum(places[LEAN], 1),
        [balanced, unbalanced],
        places, amplitudes, w, ladder, occ_energy, vir,
    )
    return lax.dynamic_update_slice_in_dim(kept, swap(sent), (1 - lax.axis_index("rep")) * TILE, 1)


def solution(mesh):
    in_specs = (P("row", "col", None), P("rep", "col", None, "row"), P(), P(), P(), P(), P())
    out_specs = P("rep", "col", None, "row")
    return jax.shard_map(body, mesh=mesh, in_specs=in_specs, out_specs=out_specs, check_vma=False)
```

```python
import functools

import jax
import jax.numpy as jnp
from jax import lax
from jax.experimental import pallas as pl
from jax.experimental.pallas import tpu as pltpu
from jax.sharding import PartitionSpec as P

TILE = 128
NX, NY, NZ, NC = 4, 4, 8, 2
NOCC, NTILE = 4, 16
AXES = ("row", "col", "rep")
OCC, TILES, PX, PY, PZ, PC = 0, 4, 20, 21, 22, 23
ORDER, KL_COUNT, LENGTHS, LEAN, KL, TILE_LIST = 24, 28, 29, 31, 32, 48
FAR_FIRST, FAR_START, FAR_COUNT, FAR_I = 80, 84, 86, 88
WINDOW = 92
ROOM = 64
W_LISTS, A_LISTS = 128, 256
NONE = 3 * ROOM
CHUNK = 8


def permutation(target):
    pairs = []
    for x in range(NX):
        for y in range(NY):
            for z in range(NZ):
                for c in range(NC):
                    tx, ty, tz, tc = target(x, y, z, c)
                    source = ((x * NY + y) * NZ + z) * NC + c
                    pairs.append((source, (((tx % NX) * NY + ty % NY) * NZ + tz % NZ) * NC + tc % NC))
    return pairs


def first_phase(v, step):
    return lax.ppermute(
        v, AXES, permutation(lambda x, y, z, c: (x, y + step, z, c) if c == 0 else (x + step, y, z, c))
    )


def second_phase(v, step):
    return lax.ppermute(
        v, AXES, permutation(lambda x, y, z, c: (x + step, y, z, c) if c == 0 else (x, y + step, z, c))
    )


def along_z(v):
    return lax.ppermute(v, AXES, permutation(lambda x, y, z, c: (x, y, z + 1 - 2 * c, c)))


def swap(v):
    return lax.ppermute(v, AXES, permutation(lambda x, y, z, c: (x, y, z, 1 - c)))


def parity(value):
    return lax.rem(value, 2)


def tiles_by_irrep(ints):
    first, end = ints[WINDOW], ints[WINDOW + 1]
    odd = jnp.int32(0)
    for tile in range(NTILE):
        odd = odd + jnp.where((tile >= first) & (tile < end), ints[TILES + tile], 0)
    return end - first - odd, odd


def count_of(counts, which):
    return jnp.where(which == 1, counts[1], counts[0])


def aligned(start):
    return pl.ds(pl.multiple_of(start * TILE, TILE), TILE)


OFFSETS = (0, 3, 1, 2)


def places_kernel(occ_irrep, tile_irrep, ints, build):
    row, z, core = (lax.axis_index(axis) for axis in AXES)
    for at, place in ((PX, lax.div(row, NY)), (PY, lax.rem(row, NY)), (PZ, z), (PC, core)):
        ints[at] = place
    total = jnp.int32(-2)
    for k in range(NOCC):
        ints[OCC + k] = occ_irrep[k]
        total = total + occ_irrep[k]
    for tile in range(NTILE):
        ints[TILES + tile] = tile_irrep[tile]
    ints[LEAN] = jnp.abs(total)
    build[0] = jnp.minimum(jnp.abs(total), 1)


def make_places(occ_irrep, tile_irrep):
    smem = pl.BlockSpec(memory_space=pltpu.SMEM)
    return pl.pallas_call(
        places_kernel,
        out_shape=(jax.ShapeDtypeStruct((LEAN + 1,), jnp.int32), jax.ShapeDtypeStruct((1,), jnp.int32)),
        in_specs=[smem, smem],
        out_specs=(smem, smem),
    )(occ_irrep, tile_irrep)


def tables_kernel(places, window, ints):
    x, y, z, core = places[PX], places[PY], places[PZ], places[PC]
    row = x * NY + y
    for at in (PX, PY, PZ, PC, OCC, OCC + 1, OCC + 2, OCC + 3):
        ints[at] = places[at]
    occ_irreps = [places[OCC + k] for k in range(NOCC)]
    common_sum = occ_irreps[0] + occ_irreps[1] + occ_irreps[2] + occ_irreps[3]

    for n in range(4):
        ints[WINDOW + n] = window[n]
    for tile in range(NTILE):
        ints[TILES + tile] = places[TILES + tile]

    def list_step(tile, ends):
        even, odd = ends
        is_odd = places[TILES + tile]
        ints[TILE_LIST + jnp.where(is_odd == 1, odd, even)] = tile
        return even + 1 - is_odd, odd + is_odd

    evens, odds = lax.fori_loop(window[0], window[1], list_step, (jnp.int32(0), jnp.int32(NTILE)))
    counts = (evens, odds - NTILE)
    tile_a = places[TILES + z * 2 + core]
    tile_b = places[TILES + row]
    here = jnp.where(core == 0, x, y)
    far = lax.rem(here + 2, 4)
    ints[FAR_I] = far

    def piece_of(distance, own_half):
        below = distance > 4
        steps = jnp.where(below, 8 - distance, distance)
        received = below == (core == 0)
        part = jnp.where(received, 1 - own_half, own_half)
        ring = jnp.where(steps == 3, jnp.where(received, 10, 13), jnp.where(received, 0, 4) + steps * 2) + part
        return jnp.where(distance == 0, 1 - own_half, jnp.where(distance == 4, 15 - 3 * own_half, ring))

    for g in range(2):
        place = jnp.int32(0)
        far_start, far_count = jnp.int32(0), jnp.int32(0)
        for k in range(NOCC):
            need = parity(occ_irreps[k] + g)
            count = count_of(counts, need)
            own_half = jnp.where(core == k // 2, 1, 0)
            far_start = jnp.where(far == k, place, far_start)
            far_count = jnp.where(far == k, count, far_count)

            def step(n, carry, place=place, first=need * NTILE, own_half=own_half, k=k, g=g):
                tile = ints[TILE_LIST + first + n]
                distance = lax.rem(lax.div(tile, 2) - z + 8, 8)
                slab = piece_of(distance, own_half) * 4 + (k % 2) * 2 + lax.rem(tile, 2)
                ints[W_LISTS + g * ROOM + place + n] = slab
                return carry

            lax.fori_loop(0, count, step, 0)
            place = place + count
        ints[LENGTHS + g] = place
        ints[FAR_START + g] = jnp.where(core == 0, 0, far_start)
        ints[FAR_COUNT + g] = jnp.where(core == 0, place, far_count)

        def clear(n, carry, g=g):
            ints[W_LISTS + g * ROOM + n] = 0
            return carry

        lax.fori_loop(place, ROOM, clear, 0)

    def entry(i, k):
        offset = jnp.int32(0)
        oi, ok = ints[OCC + i], ints[OCC + k]
        for v in range(NOCC - 1):
            with_i = count_of(counts, parity(oi + occ_irreps[v] + tile_a))
            with_k = count_of(counts, parity(ok + occ_irreps[v] + tile_a))
            offset = offset + jnp.where(core == 0, jnp.where(v < k, with_i, 0), jnp.where(v < i, with_k, 0))
        distance = lax.rem(jnp.where(core == 0, i, k) - here + 4, 4)
        block = jnp.where(distance == 0, 0, jnp.where(distance == 3, 1, jnp.where(distance == 1, 2, 3)))
        return block * ROOM + offset

    rank = jnp.int32(0)
    for tile in range(NTILE - 1):
        rank = rank + jnp.where((tile >= window[0]) & (tile < row) & (places[TILES + tile] == tile_b), 1, 0)

    def fill(i, kl_count):
        place = jnp.int32(0)
        far_first = jnp.int32(0)
        for k in range(NOCC):
            first = entry(i, k)
            need = parity(ints[OCC + i] + occ_irreps[k] + tile_a)
            count = count_of(counts, need)
            far_first = jnp.where((far == k) & (core == 1), first - NONE, far_first)

            def step(n, carry, place=place, first=first):
                ints[A_LISTS + i * ROOM + place + n] = first + n
                return carry

            lax.fori_loop(0, count, step, 0)
            place = place + count
            hit = (need == tile_b) & (row >= window[0]) & (row < window[1])

            @pl.when(hit)
            def _(first=first, k=k, kl_count=kl_count):
                ints[KL + kl_count] = (i * NOCC + k) * 256 + first + rank

            kl_count = kl_count + jnp.where(hit, 1, 0)
        ints[FAR_FIRST + i] = far_first

        def clear(n, carry):
            ints[A_LISTS + i * ROOM + n] = NONE
            return carry

        lax.fori_loop(place, ROOM, clear, 0)
        return kl_count

    ints[KL_COUNT] = lax.fori_loop(0, NOCC, fill, jnp.int32(0))
    common = jnp.where(common_sum > 2, 1, 0)
    place = jnp.int32(0)
    for irrep in (common, 1 - common):
        for i in range(NOCC):
            hit = occ_irreps[i] == irrep

            @pl.when(hit)
            def _(place=place, i=i):
                ints[ORDER + place] = i

            place = place + jnp.where(hit, 1, 0)


def make_tables(places, window):
    smem = pl.BlockSpec(memory_space=pltpu.SMEM)
    return pl.pallas_call(
        tables_kernel,
        out_shape=jax.ShapeDtypeStruct((A_LISTS + NOCC * ROOM,), jnp.int32),
        in_specs=[smem, smem],
        out_specs=smem,
    )(places, window)


def pack_kernel(ints, own, ahead, behind, far, out):
    core = ints[PC]
    tile_counts = tiles_by_irrep(ints)
    here = jnp.where(core == 0, ints[PY], ints[PX])
    fixed = jnp.where(core == 0, ints[PX], ints[PY])
    side = ints[OCC + fixed] + ints[TILES + ints[PZ] * 2 + core]
    counts = [count_of(tile_counts, parity(side + ints[OCC + v])) for v in range(NOCC)]
    for offset, buffer in zip(OFFSETS, (own, ahead, behind, far)):
        v = lax.rem(here + offset, 4)
        need = parity(side + ints[OCC + v])
        base = jnp.int32(0)
        for w in range(NOCC - 1):
            base = base + jnp.where(w < v, counts[w], 0)

        def step(n, carry, buffer=buffer, base=base, first=need * NTILE):
            out[:, aligned(base + n)] = buffer[:, aligned(ints[TILE_LIST + first + n])]
            return carry

        lax.fori_loop(0, count_of(tile_counts, need), step, 0)


def pack(cap, ints, own, ahead, behind, far):
    vmem = pl.BlockSpec(memory_space=pltpu.VMEM)
    return pl.pallas_call(
        pack_kernel,
        out_shape=jax.ShapeDtypeStruct((TILE, cap * TILE), jnp.bfloat16),
        in_specs=[pl.BlockSpec(memory_space=pltpu.SMEM)] + [vmem] * 4,
        out_specs=vmem,
        compiler_params=pltpu.CompilerParams(vmem_limit_bytes=8 << 20),
        cost_estimate=pl.CostEstimate(flops=1 << 20, bytes_accessed=1 << 16, transcendentals=0),
    )(ints, own, ahead, behind, far)


def pack_cycle_kernel(cap_j, ints, window, w, out):
    core, z = ints[PC], ints[PZ]
    right = ints[TILES + ints[PX] * NY + ints[PY]]
    for k in range(2):
        for tile in range(2):
            need = parity(ints[OCC + core * 2 + k] + ints[TILES + z * 2 + tile] + right)
            rows = slice((k * 2 + tile) * TILE, (k * 2 + tile + 1) * TILE)
            if cap_j > 2:
                out[rows, :] = jnp.zeros((TILE, cap_j * TILE), jnp.bfloat16)
            place = jnp.int32(0)
            for j in range(NOCC):
                hit = (ints[OCC + j] == need) & (j >= window[2]) & (j < window[3])

                @pl.when(hit)
                def _(place=place, j=j, k=k, tile=tile, rows=rows):
                    out[rows, aligned(place)] = w[k, j, tile * TILE : (tile + 1) * TILE, :]

                place = place + jnp.where(hit, 1, 0)


def pack_cycle(cap_j, ints, window, w):
    vmem = pl.BlockSpec(memory_space=pltpu.VMEM)
    smem = pl.BlockSpec(memory_space=pltpu.SMEM)
    return pl.pallas_call(
        functools.partial(pack_cycle_kernel, cap_j),
        out_shape=jax.ShapeDtypeStruct((4 * TILE, cap_j * TILE), jnp.bfloat16),
        in_specs=[smem, smem, vmem],
        out_specs=vmem,
        compiler_params=pltpu.CompilerParams(vmem_limit_bytes=4 << 20),
    )(ints, window, w)


def near_kernel(cap_j, ints, a_near, w_all, acc):
    def product(rows):
        g = parity(ints[OCC + rows[0]] + ints[TILES + ints[PZ] * 2 + ints[PC]])

        def a_tile(i, n):
            at = ints[A_LISTS + i * ROOM + n]
            block = lax.div(at, ROOM)
            tile = a_near[aligned(jnp.minimum(block, 2)), aligned(jnp.where(block == 3, 0, lax.rem(at, ROOM)))]
            return jnp.where(block == 3, jnp.zeros_like(tile), tile)

        def step(n, total):
            lefts, rights = [], []
            for part in range(CHUNK):
                at = n * CHUNK + part
                lefts.append(jnp.concatenate([a_tile(i, at) for i in rows], axis=0))
                rights.append(w_all[aligned(ints[W_LISTS + g * ROOM + at]), :])
            return total + jnp.dot(
                jnp.concatenate(lefts, axis=1),
                jnp.concatenate(rights, axis=0),
                preferred_element_type=jnp.float32,
            )

        total = lax.fori_loop(
            0,
            lax.div(ints[LENGTHS + g] + CHUNK - 1, CHUNK),
            step,
            jnp.zeros((len(rows) * TILE, cap_j * TILE), jnp.float32),
        )
        for at, i in enumerate(rows):
            acc[i] = total[at * TILE : (at + 1) * TILE]

    for_groups(cap_j, ints, product)


def for_groups(cap_j, ints, product):
    def single(n, carry):
        product([ints[ORDER + n]])
        return carry

    def pair(n, carry):
        product([ints[ORDER + 2 * n], ints[ORDER + 2 * n + 1]])
        return carry

    if cap_j == 2:
        lax.fori_loop(0, 2, pair, 0)
    else:
        product([ints[ORDER], ints[ORDER + 1]])
        lax.fori_loop(2, NOCC, single, 0)


def far_kernel(cap_j, ints, ladder, occ, vir, a_near, a_far, w_all, acc_in, *refs):
    earlier, (kept, sent, acc, tiles) = refs[:-4], refs[-4:]
    core, z = ints[PC], ints[PZ]
    tile_a_at, tile_b_at = z * 2 + core, ints[PX] * NY + ints[PY]
    tile_a, tile_b = ints[TILES + tile_a_at], ints[TILES + tile_b_at]
    occ_irreps = [ints[OCC + k] for k in range(NOCC)]
    acc[...] = acc_in[...]

    def product(rows):
        g = parity(ints[OCC + rows[0]] + tile_a)
        first, count = ints[FAR_START + g], ints[FAR_COUNT + g]

        def add(begin, size):
            lefts, rights = [], []
            for part in range(size):
                lefts.append(
                    jnp.concatenate([a_far[:, aligned(ints[FAR_FIRST + i] + begin + part)] for i in rows], axis=0)
                )
                rights.append(w_all[aligned(ints[W_LISTS + g * ROOM + first + begin + part]), :])
            total = jnp.dot(
                jnp.concatenate(lefts, axis=1),
                jnp.concatenate(rights, axis=0),
                preferred_element_type=jnp.float32,
            )
            for at, i in enumerate(rows):
                acc[i] += total[at * TILE : (at + 1) * TILE]

        whole = lax.div(count, 4)

        def by_four(n, carry):
            add(n * 4, 4)
            return carry

        def by_one(n, carry):
            add(n, 1)
            return carry

        lax.fori_loop(0, whole, by_four, 0)
        lax.fori_loop(whole * 4, count, by_one, 0)

    @pl.when(core == 0)
    def _():
        product([ints[FAR_I]])

    @pl.when(core == 1)
    def _():
        for_groups(cap_j, ints, product)

    kl_count = ints[KL_COUNT]

    def keep_tile(n, carry):
        at = lax.rem(ints[KL + n], 256)
        block, columns = lax.div(at, ROOM), aligned(lax.rem(at, ROOM))
        near = a_near[aligned(jnp.minimum(block, 2)), columns]
        tiles[n] = jnp.where(block == 3, a_far[:, columns], near).astype(jnp.float32)
        return carry

    lax.fori_loop(0, kl_count, keep_tile, 0)
    vir_b = vir[pl.ds(tile_b_at, 1), :]
    vir_a = jnp.broadcast_to(vir[pl.ds(tile_a_at, 1), :], (TILE, TILE)).T

    is_first = (ints[WINDOW] == 0) & (ints[WINDOW + 2] == 0)
    for side, (out, begin, at) in enumerate(((kept, core * 2, core * TILE), (sent, 2 - core * 2, 0))):
        rows = pl.ds(pl.multiple_of(at, TILE), TILE)

        def finish(ii, carry, side=side, out=out, begin=begin, rows=rows):
            i = begin + ii
            need = parity(ints[OCC + i] + tile_a + tile_b)
            place = jnp.int32(0)
            for j in range(NOCC):
                hit = (occ_irreps[j] == need) & (j >= ints[WINDOW + 2]) & (j < ints[WINDOW + 3])

                @pl.when(hit)
                def _(j=j, place=place):
                    def add(n, total):
                        return total + ladder[i * NOCC + j, lax.div(ints[KL + n], 256)] * tiles[n]

                    total = lax.fori_loop(0, kl_count, add, acc[i, :, aligned(place)])
                    out[ii, rows, j, :] = total / (((occ[i] - vir_a) + occ[j]) - vir_b)

                @pl.when(jnp.logical_not(hit))
                def _(j=j):
                    out[ii, rows, j, :] = jnp.zeros((TILE, TILE), jnp.float32)

                if earlier:

                    @pl.when(jnp.logical_not(is_first))
                    def _(j=j):
                        out[ii, rows, j, :] += earlier[side][ii, rows, j, :]

                place = place + jnp.where(hit, 1, 0)
            return carry

        lax.fori_loop(0, 2, finish, 0)


OUT_SHAPES = tuple(jax.ShapeDtypeStruct((2, rows, NOCC, TILE), jnp.float32) for rows in (2 * TILE, TILE))


def products(cap, cap_j, ints, ladder, occ, vir, a_near, a_far, w_all, earlier):
    vmem = pl.BlockSpec(memory_space=pltpu.VMEM)
    smem = pl.BlockSpec(memory_space=pltpu.SMEM)
    sums = (NOCC, TILE, cap_j * TILE)
    limit = (14 << 20) * cap // 32
    acc = pl.pallas_call(
        functools.partial(near_kernel, cap_j),
        out_shape=jax.ShapeDtypeStruct(sums, jnp.float32),
        in_specs=[smem, vmem, vmem],
        out_specs=vmem,
        compiler_params=pltpu.CompilerParams(vmem_limit_bytes=limit),
        cost_estimate=pl.CostEstimate(flops=1 << 20, bytes_accessed=1 << 16, transcendentals=0),
    )(ints, a_near, w_all)
    return pl.pallas_call(
        functools.partial(far_kernel, cap_j),
        out_shape=OUT_SHAPES,
        in_specs=[smem, smem, smem] + [vmem] * (5 + len(earlier)),
        out_specs=(vmem, vmem),
        scratch_shapes=[pltpu.VMEM(sums, jnp.float32), pltpu.VMEM((16, TILE, TILE), jnp.float32)],
        compiler_params=pltpu.CompilerParams(vmem_limit_bytes=limit + (4 << 20)),
        cost_estimate=pl.CostEstimate(flops=1 << 20, bytes_accessed=1 << 16, transcendentals=0),
    )(ints, ladder, occ, vir, a_near, a_far, w_all, acc, *earlier)


def own_rows(amplitudes):
    return lax.dynamic_slice_in_dim(amplitudes[0], lax.axis_index("rep") * TILE, TILE, 0)


def planned(cap, cap_j, earlier, window, places, amplitudes, w, ladder, occ, vir):
    own = own_rows(amplitudes)
    ahead, behind, far = first_phase(own, 1), first_phase(own, -1), first_phase(own, 2)

    mine = pack_cycle(cap_j, places, window, w)
    other = swap(mine)
    ring = []
    first, second = mine, other
    ints = make_tables(places, window)
    for step in range(3):
        if step == 1:
            first, second, ints = lax.optimization_barrier((first, second, ints))
        first, second = along_z(first), along_z(second)
        ring += [first, second]
    ring.append(along_z(first))

    packed = pack(cap, ints, own, ahead, behind, far)
    a_near = jnp.concatenate([packed, second_phase(packed, 1), second_phase(packed, -1)])
    a_far = second_phase(packed, 2)

    near, further = jnp.concatenate(ring[:4]), jnp.concatenate(ring[4:])
    further, a_far = lax.optimization_barrier((further, a_far))
    w_all = jnp.concatenate([mine, other, near, swap(near), further, swap(further)])
    ladder = lax.optimization_barrier((ladder, packed))[0].astype(jnp.float32)
    return products(cap, cap_j, ints, ladder, occ, vir, a_near, a_far, w_all, earlier)


def balanced(*operands):
    return planned(32, 2, (), jnp.array([0, NTILE, 0, NOCC], jnp.int32), *operands)


def unbalanced(places, *operands):
    even_split = places[LEAN] == 2

    def one_pass(n, earlier):
        c, j = n % 2 * (NTILE // 2), n // 2 * 2
        window = jnp.where(
            even_split, jnp.stack([c, c + NTILE // 2, j, j + 2]), jnp.array([0, NTILE, 0, NOCC], jnp.int32)
        )
        return planned(48, 3, earlier, window.astype(jnp.int32), places, *operands)

    space = pl.BlockSpec(memory_space=pl.ANY)
    unset = pl.pallas_call(lambda kept, sent: None, out_shape=OUT_SHAPES, out_specs=(space, space))()
    return lax.fori_loop(0, jnp.where(even_split, 4, 1), one_pass, tuple(unset))


def body(
    amplitudes, cycle_integrals, ladder_integrals, occ_energy, vir_energy, occ_irrep, tile_irrep
):
    w = cycle_integrals.transpose(0, 2, 1, 3)
    vir = vir_energy.reshape(NTILE, TILE)
    places, build = make_places(occ_irrep, tile_irrep)
    kept, sent = lax.switch(
        build.reshape(()),
        [balanced, unbalanced],
        places, amplitudes, w, ladder_integrals, occ_energy, vir,
    )
    return lax.dynamic_update_slice_in_dim(kept, swap(sent), (1 - lax.axis_index("rep")) * TILE, 1)


def solution(mesh):
    in_specs = (P("row", "col", None), P("rep", "col", None, "row"), P(), P(), P(), P(), P())
    out_specs = P("rep", "col", None, "row")
    return jax.shard_map(body, mesh=mesh, in_specs=in_specs, out_specs=out_specs, check_vma=False)
```
